32 devices in a mesh: blk: 8 (over z, y), trk: 4 (over x, core).
Axes of the slice: x: 2, y: 2, z: 4, core: 2. Of those that a mesh axis runs over, the one named last changes fastest.
Arguments:
- row_block: int32 [8192, 1], P(('blk', 'trk')), may hold values from 0 to 7; in each aligned block of 256 rows (0 to 255, 256 to 511, ...) at most 64 rows name the same one
- row_hits: int32 [2, 8192], P(None, ('blk', 'trk')), may hold values from 0 to 63
- row_slot: int32 [8192], P(('blk', 'trk')), may hold values from 0 to 4
- track_kept: int32 [1024], P(('blk', 'trk')), may hold values 0 or 1
- row_derivs: bfloat16 [12, 8192], P(None, ('blk', 'trk')), may hold values from -0.75 to 0.75
- row_resid: bfloat16 [8192], P(('blk', 'trk')), may hold values from -6 to 6
- row_invsig: bfloat16 [8192], P(('blk', 'trk')), may hold values from 0.5 to 2
- pattern: int32 [8, 5], P('blk'), may hold values from 0 to 7, as said below
- prior: float32 [8, 384], P('blk'), may hold values from 0.2 to 3
Outputs:
- solution: float32 [8, 384], P('blk')
- gradient: float32 [8, 384], P('blk')
The draws below stay inside these ranges and needn't reach their ends.
Inputs may be any that keep to these rules, and one draw needn't show every extreme that they name: `row_block`: among the rows of one device (aligned blocks of 256 rows) no block is named by more than 64 rows, and in every draw some device's rows name some block exactly 64 times. `pattern`: row k lists the blocks k - 2, k - 1, k, k + 1, k + 2 modulo 8, each once, in an order of its own.
All inputs are finite; a program needn't handle non-finite values. No bound on the sum of `track_kept` on one device may be relied on, other than what follows from the above.
Results may differ from the reference program's by a relative error of at most 0.0036.
The reference program's roundings to bfloat16 on the way (of `scaled` and `weighted`) count: a program that leaves them out, or rounds other values in their place, can miss the bound.
Values may be sent and summed in bfloat16 or wider, within the bound.
A program may use at most 64 MiB of HBM per device.

```python
import math
import jax
import jax.numpy as jnp
import numpy as np
from jax import lax

MODS = 64
PAR = 6
NB = 5
SEG = 8
ITERS = 2
ROW_DEV = 256
ORDER = 384
NBLK = 8
CAP = 64
ROWS = 8192
TRACKS = 1024


def draw_pattern(key, part):
    keys = jax.random.split(key, NBLK)
    orders = jax.vmap(lambda one_key: jax.random.permutation(one_key, NB))(keys)
    offsets = orders.astype(jnp.int32) - NB // 2
    return (jnp.arange(NBLK, dtype=jnp.int32)[:, None] + offsets) % NBLK


def draw_prior(key, part):
    position = jnp.arange(NBLK, dtype=jnp.float32)[:, None] / max(NBLK - 1, 1)
    rising = 1.0 + 2.0 * position
    base = jnp.exp(jax.random.uniform(key, (NBLK, ORDER), jnp.float32, math.log(0.2), 0.0))
    return base * rising


def with_ends(result, key, low, top_value):
    dims = result.shape
    place = [jax.random.randint(jax.random.fold_in(key, axis), (), 0, dims[axis]) for axis in range(len(dims))]
    result = result.at[tuple(place)].set(low)
    longest = dims.index(max(dims))
    place[longest] = (place[longest] + 1) % dims[longest]
    return result.at[tuple(place)].set(top_value)


def block_scale(key, extent, cuts, least, high):
    factor_of, own = 1.0, jax.random.fold_in(key, 6)
    for dim, parts in cuts:
        draws = jnp.exp(jax.random.uniform(jax.random.fold_in(own, dim), (parts,), jnp.float32, least / len(cuts), high / len(cuts)))
        factor_of = factor_of * jnp.repeat(draws, extent[dim] // parts).reshape([-1 if axis == dim else 1 for axis in range(len(extent))])
    return factor_of


def routed_block(own_key, own, number, rows, number_of, top, reach, skew):
    sequence = jax.random.permutation(own_key, number_of)
    crowded, usual = shares(number_of, rows * top, reach, skew, True), shares(number_of, rows * top, reach, skew, False)
    places = jnp.arange(number_of)

    def named(lengths, offset_by):
        used = int((lengths > 0).sum())
        fixed = max(1, used // 4)
        shifted = fixed + (places - fixed + offset_by * (used - fixed)) % max(1, number_of - fixed)
        return jnp.zeros((number_of,), jnp.int32).at[sequence[jnp.where(places < fixed, places, shifted)]].set(jnp.asarray(lengths, jnp.int32))

    lengths = jnp.where(number % 4 == 0, named(crowded, number // 4), named(usual, number - number // 4 - 1))
    mixed = jax.random.permutation(jax.random.fold_in(own, 3), number_of)
    donor, taker = mixed[0:number_of // 2 * 2:2], mixed[1:number_of // 2 * 2:2]
    margin = jnp.minimum(lengths[donor] - 1, reach - lengths[taker]) // 2
    margin = jnp.where((donor == sequence[0]) | (taker == sequence[0]) | (lengths[taker] == 0), 0, jnp.maximum(margin, 0))
    shifted = jax.random.randint(jax.random.fold_in(own, 4), (number_of // 2,), 0, 1 << 20) % (margin + 1)
    lengths = lengths.at[donor].add(-shifted).at[taker].add(shifted)
    items = jnp.searchsorted(jnp.cumsum(lengths), jnp.arange(rows * top), side="right").astype(jnp.int32)
    table = items.reshape(top, rows).T
    table = table[jax.random.permutation(jax.random.fold_in(own, 1), rows)]
    offset_by = jax.random.randint(jax.random.fold_in(own, 2), (rows, 1), 0, top)
    return jnp.take_along_axis(table, (jnp.arange(top)[None, :] + offset_by) % top, axis=1)


def shares(count, total, reach, slope, full):
    portions = [(1 << 20) // math.isqrt(rank ** slope) + 1 for rank in range(1, count + 1)]
    largest = reach if full else min(reach, max(-(-total // count), total * portions[0] // sum(portions)))
    least = 1 if total - largest >= count - 1 else 0
    holding, spare = [largest] + [least] * (count - 1), total - largest - least * (count - 1)
    while spare > 0:
        movable = [i for i in range(1, count) if holding[i] < largest] or [i for i in range(1, count) if holding[i] < reach]
        whole, left = sum([portions[i] for i in movable]), spare
        for i in movable:
            more = min(reach - holding[i], max(1, left * portions[i] // whole), spare)
            holding[i] = holding[i] + more
            spare = spare - more
    return np.array(holding)


def normal_values(key, dims, scale, most, shards=(), kind=jnp.bfloat16):
    result = scale * jax.random.normal(key, dims, jnp.float32)
    if shards:
        result = result * block_scale(key, dims, shards, -0.22, 0.18)
    return jnp.clip(result, -most, most).astype(kind)


def setup_inputs(seed: int = 0) -> dict:
    streams_of = jax.random.split(jax.random.key(seed), 10)
    row_block_keys = jax.random.split(jax.random.fold_in(streams_of[0], 1), ROWS // ROW_DEV)
    row_block_turns = jax.random.permutation(jax.random.fold_in(streams_of[0], 3), ROWS // ROW_DEV)
    row_block = jax.vmap(lambda own, number: routed_block(jax.random.fold_in(streams_of[0], 2), own, number, ROW_DEV, NBLK, 1, CAP, 2))(row_block_keys, row_block_turns).reshape((ROWS, 1))
    row_hits = with_ends(jax.random.randint(streams_of[1], (2, ROWS), 0, MODS), jax.random.fold_in(streams_of[1], 1), 0, MODS - 1).astype(jnp.int32)
    row_slot = with_ends(jax.random.randint(streams_of[2], (ROWS,), 0, NB), jax.random.fold_in(streams_of[2], 1), 0, NB - 1).astype(jnp.int32)
    track_kept = with_ends((jax.random.randint(streams_of[3], (TRACKS,), 0, 4) < 3).astype(jnp.int32), jax.random.fold_in(streams_of[3], 1), 0, 1)
    row_derivs = normal_values(streams_of[4], (2 * PAR, ROWS), 0.125, 0.75, ((1, 32),))
    row_resid = normal_values(streams_of[5], (ROWS,), 1.0, 6.0, ((0, 32),))
    row_invsig = jnp.clip(jnp.exp(math.log(2.0) - 1.3862944 * jax.random.uniform(streams_of[6], (ROWS,), jnp.float32) ** block_scale(streams_of[6], (ROWS,), ((0, 32),), -0.2, 0.2)), 0.5, 2.0).astype(jnp.bfloat16)
    pattern = draw_pattern(jax.random.fold_in(streams_of[9], 71), 0)
    prior = draw_prior(jax.random.fold_in(streams_of[9], 71), 0)
    return dict(row_block=row_block, row_hits=row_hits, row_slot=row_slot, track_kept=track_kept, row_derivs=row_derivs, row_resid=row_resid, row_invsig=row_invsig, pattern=pattern, prior=prior)


epsilon = 1e-06

def rounded(value):
    return lax.optimization_barrier(value.astype(jnp.bfloat16)).astype(jnp.float32)

def project(initial_norm, diag_terms, off_terms, basis_list):
    size_count = len(diag_terms)
    zero_value = diag_terms[0] * 0.0
    rows_list = []
    for row_index in range(size_count + 1):
        entries = []
        for column in range(size_count):
            if row_index == column:
                entries.append(diag_terms[column])
            elif row_index == column + 1:
                entries.append(off_terms[column])
            elif column == row_index + 1:
                entries.append(off_terms[row_index])
            else:
                entries.append(zero_value)
        rows_list.append(jnp.stack(entries))
    tridiagonal = jnp.stack(rows_list)
    gram_matrix = jnp.dot(tridiagonal.T, tridiagonal, precision=lax.Precision.HIGHEST)
    target = initial_norm * tridiagonal[0]
    factor = jnp.linalg.cholesky(gram_matrix)
    forward = []
    for row_index in range(size_count):
        partial_sum = target[row_index]
        for column in range(row_index):
            partial_sum = partial_sum - factor[row_index, column] * forward[column]
        forward.append(partial_sum / factor[row_index, row_index])
    backward = [zero_value] * size_count
    for row_index in reversed(range(size_count)):
        partial_sum = forward[row_index]
        for column in range(row_index + 1, size_count):
            partial_sum = partial_sum - factor[column, row_index] * backward[column]
        backward[row_index] = partial_sum / factor[row_index, row_index]
    solution = backward[0] * basis_list[0]
    for row_index in range(1, size_count):
        solution = solution + backward[row_index] * basis_list[row_index]
    return solution

def reference(row_block, row_hits, row_slot, track_kept, row_derivs, row_resid, row_invsig, pattern, prior):
    kept_rows = jnp.repeat(track_kept, SEG).astype(jnp.float32)
    scaling = kept_rows * row_invsig.astype(jnp.float32)
    scaled = rounded(scaling[None, :] * row_derivs.astype(jnp.float32))
    weighted = rounded(scaling * row_resid.astype(jnp.float32))
    first_block = row_block[:, 0].astype(jnp.int32)
    second_block = pattern[first_block, row_slot].astype(jnp.int32)
    first_module = (first_block * MODS + row_hits[0]).astype(jnp.int32)
    second_module = (second_block * MODS + row_hits[1]).astype(jnp.int32)
    first_der = scaled[:PAR].T
    second_der = scaled[PAR:].T
    module_count = NBLK * MODS

    def spread(first_values, second_values):
        summed = jax.ops.segment_sum(first_values, first_module, num_segments=module_count)
        summed = summed + jax.ops.segment_sum(second_values, second_module, num_segments=module_count)
        return summed.reshape(NBLK, ORDER)

    def operate(vector_in):
        flat_field = vector_in.reshape(module_count, PAR)
        along_row = lax.optimization_barrier(jnp.sum(first_der * flat_field[first_module], axis=1))
        along_row = along_row + lax.optimization_barrier(jnp.sum(second_der * flat_field[second_module], axis=1))
        return prior * vector_in + spread(first_der * along_row[:, None], second_der * along_row[:, None])
    gradient = spread(first_der * weighted[:, None], second_der * weighted[:, None])
    initial_norm = jnp.sqrt(jnp.sum(gradient * gradient) + epsilon)
    current = gradient / initial_norm
    previous = jnp.zeros_like(gradient)
    beta_term = jnp.zeros((), jnp.float32)
    diag_terms, off_terms, basis_list = ([], [], [])
    for iteration in range(ITERS):
        image_vec = operate(current)
        alpha_term = jnp.sum(current * image_vec)
        direction = image_vec - alpha_term * current - beta_term * previous
        beta_next = jnp.sqrt(jnp.sum(direction * direction) + epsilon)
        diag_terms.append(alpha_term)
        off_terms.append(beta_next)
        basis_list.append(current)
        previous, current, beta_term = (current, direction / beta_next, beta_next)
    solution = project(initial_norm, diag_terms, off_terms, basis_list)
    return (solution, gradient)
```

```python
import functools

import jax
import jax.numpy as jnp
from jax import lax
from jax.experimental import pallas as pl
from jax.experimental.pallas import tpu as pltpu
from jax.sharding import PartitionSpec as P

MODS = 64
PAR = 6
NB = 5
SEG = 8
ITERS = 2


epsilon = 1e-06


def passed_along(block, axis, distance):
    devices = range(lax.axis_size(axis))
    route = [((i - distance) % len(devices), i) for i in devices]
    return lax.ppermute(block, axis, route)


def project(initial_norm, diag_terms, off_terms, basis_list):
    size_count = len(diag_terms)
    zero_value = diag_terms[0] * 0.0
    rows_list = []
    for row_index in range(size_count + 1):
        entries = []
        for column in range(size_count):
            if row_index == column:
                entries.append(diag_terms[column])
            elif row_index == column + 1:
                entries.append(off_terms[column])
            elif column == row_index + 1:
                entries.append(off_terms[row_index])
            else:
                entries.append(zero_value)
        rows_list.append(jnp.stack(entries))
    tridiagonal = jnp.stack(rows_list)
    gram_matrix = jnp.dot(tridiagonal.T, tridiagonal, precision=lax.Precision.HIGHEST)
    target = initial_norm * tridiagonal[0]
    factor = jnp.linalg.cholesky(gram_matrix)
    forward = []
    for row_index in range(size_count):
        partial_sum = target[row_index]
        for column in range(row_index):
            partial_sum = partial_sum - factor[row_index, column] * forward[column]
        forward.append(partial_sum / factor[row_index, row_index])
    backward = [zero_value] * size_count
    for row_index in reversed(range(size_count)):
        partial_sum = forward[row_index]
        for column in range(row_index + 1, size_count):
            partial_sum = partial_sum - factor[column, row_index] * backward[column]
        backward[row_index] = partial_sum / factor[row_index, row_index]
    solution = backward[0] * basis_list[0]
    row_index = 1
    solution = solution + backward[row_index] * basis_list[row_index]
    return solution


def contract(left_rows, right_rows):
    return lax.dot_general(
        left_rows, right_rows, (((0,), (0,)), ((), ())), preferred_element_type=jnp.float32
    )


def on_device_large(
    row_block, row_hits, row_slot, track_kept, row_derivs, row_resid, row_invsig, pattern, prior
):
    row_count = row_resid.shape[0]
    owners = lax.axis_size("blk")
    capacity = 2 * row_count // owners
    order_size = MODS * PAR
    kept_rows = jnp.repeat(track_kept, SEG).astype(jnp.float32)
    scaling = kept_rows * row_invsig.astype(jnp.float32)
    scaled = (scaling[None, :] * row_derivs.astype(jnp.float32)).astype(jnp.bfloat16)
    weighted = (scaling * row_resid.astype(jnp.float32)).astype(jnp.bfloat16)
    destination = row_block[:, 0]
    member = (destination[:, None] == jnp.arange(owners, dtype=jnp.int32)[None, :]).astype(
        jnp.bfloat16
    )
    row_ids = jnp.arange(row_count, dtype=jnp.int32)
    earlier = (row_ids[:, None] > row_ids[None, :]).astype(jnp.bfloat16)
    before = jnp.dot(earlier, member, preferred_element_type=jnp.float32)
    rank_within = jnp.sum(before * member.astype(jnp.float32), axis=1).astype(jnp.int32)
    slot_place = destination * capacity + rank_within
    labels = jnp.stack([row_hits[0], row_hits[1], row_slot]).astype(jnp.bfloat16)
    record = jnp.concatenate([scaled, weighted[None, :], labels], axis=0)
    outgoing = (
        jnp.zeros((record.shape[0], owners * capacity), jnp.bfloat16).at[:, slot_place].set(record)
    )
    incoming = lax.all_to_all(outgoing, "blk", split_axis=1, concat_axis=1, tiled=True)
    column_ids = jnp.arange(order_size, dtype=jnp.int32)
    column_module = column_ids // PAR
    column_param = column_ids % PAR

    def expand(values, module_ids):
        spread = jnp.zeros((values.shape[1], order_size), jnp.bfloat16)
        for component in range(PAR):
            spread = jnp.where(
                column_param[None, :] == component, values[component][:, None], spread
            )
        return jnp.where(
            module_ids[:, None] == column_module[None, :], spread, jnp.zeros_like(spread)
        )

    first_module = incoming[2 * PAR + 1].astype(jnp.int32)
    second_module = incoming[2 * PAR + 2].astype(jnp.int32)
    slot_in = incoming[2 * PAR + 3].astype(jnp.int32)
    resid_in = incoming[2 * PAR]
    first_rows = expand(incoming[0:PAR], first_module)
    second_rows = expand(incoming[PAR : 2 * PAR], second_module)
    own_block = contract(first_rows, first_rows)
    grad_own = jnp.dot(resid_in, first_rows, preferred_element_type=jnp.float32)
    cross_list, partner_list, grad_list = ([], [], [])
    for slot_id in range(NB):
        masked = jnp.where((slot_in == slot_id)[:, None], second_rows, jnp.zeros_like(second_rows))
        cross_list.append(contract(first_rows, masked))
        partner_list.append(contract(masked, masked))
        grad_list.append(jnp.dot(resid_in, masked, preferred_element_type=jnp.float32))
    cross_blocks = jnp.stack(cross_list)
    partner_blocks = jnp.stack(partner_list)
    grad_partner = jnp.stack(grad_list)
    position = lax.axis_index("blk")
    neighbours = pattern[0]
    offset = (neighbours - position) % owners
    offset = jnp.where(offset > owners // 2, offset - owners, offset)

    def deliver(own_term, partner_terms):
        local_sum = own_term + jnp.sum(
            jnp.where((offset == 0)[:, None], partner_terms, 0.0), axis=0, keepdims=True
        )
        for shift_by in (-2, -1, 1, 2):
            sending = jnp.sum(
                jnp.where((offset == shift_by)[:, None], partner_terms, 0.0), axis=0, keepdims=True
            )
            local_sum = local_sum + passed_along(sending, "blk", shift_by)
        return lax.psum(local_sum, "trk")

    gradient = deliver(grad_own[None, :], grad_partner)
    initial_norm = jnp.sqrt(lax.psum(jnp.sum(gradient * gradient), "blk") + epsilon)
    current = gradient / initial_norm
    previous = jnp.zeros_like(gradient)
    beta_term = jnp.zeros((), jnp.float32)
    diag_terms, off_terms, basis_list = ([], [], [])
    for iteration in range(ITERS):
        result = jnp.where((offset == 0)[:, None], current, 0.0)
        for fetch_shift_by in (-2, -1, 1, 2):
            arrived = passed_along(current, "blk", -fetch_shift_by)
            result = result + jnp.where((offset == fetch_shift_by)[:, None], arrived, 0.0)
        operate_own_term = jnp.dot(own_block, current[0], precision=lax.Precision.HIGHEST)
        operate_own_term = operate_own_term + jnp.einsum(
            "kij,kj->i", cross_blocks, result, precision=lax.Precision.HIGHEST
        )
        operate_partner_terms = jnp.einsum(
            "kij,i->kj", cross_blocks, current[0], precision=lax.Precision.HIGHEST
        )
        operate_partner_terms = operate_partner_terms + jnp.einsum(
            "kij,kj->ki", partner_blocks, result, precision=lax.Precision.HIGHEST
        )
        image_vec = prior * current + deliver(operate_own_term[None, :], operate_partner_terms)
        alpha_term = lax.psum(jnp.sum(current * image_vec), "blk")
        direction = image_vec - alpha_term * current - beta_term * previous
        beta_next = jnp.sqrt(lax.psum(jnp.sum(direction * direction), "blk") + epsilon)
        diag_terms.append(alpha_term)
        off_terms.append(beta_next)
        basis_list.append(current)
        previous, current, beta_term = (current, direction / beta_next, beta_next)
    solution = project(initial_norm, diag_terms, off_terms, basis_list)
    return (solution, gradient)


LANES = 128
WIDE = 8
PHASES = ITERS + 1


def two_parts(value):
    high = value.astype(jnp.bfloat16)
    low = (value - high.astype(jnp.float32)).astype(jnp.bfloat16)
    return jnp.concatenate([high, low], axis=0)


def three_parts(value):
    high = value.astype(jnp.bfloat16).astype(jnp.float32)
    rest = value - high
    middle = rest.astype(jnp.bfloat16).astype(jnp.float32)
    return jnp.concatenate([high, middle, rest - middle], axis=0).astype(jnp.bfloat16)


def total(value):
    return jnp.sum(jnp.sum(value, axis=0, keepdims=True), axis=1, keepdims=True)


def kernel(
    owners,
    shares,
    block_ref,
    hits_ref,
    slot_ref,
    kept_ref,
    derivs_ref,
    resid_ref,
    invsig_ref,
    pattern_ref,
    prior_ref,
    out_ref,
    onehot,
    table,
    part,
    landed,
    blocks,
    full,
    table_send,
    table_recv,
    part_send,
    part_recv,
    block_send,
    block_recv,
    full_send,
    full_recv,
):
    blk, trk = lax.axis_index("blk"), lax.axis_index("trk")
    rows = block_ref.shape[1]
    tracks = kept_ref.shape[1]
    modules = owners * MODS
    order_size = MODS * PAR
    per_share = LANES // MODS

    def other_blk(distance):
        return {"blk": lax.rem(blk + distance, owners), "trk": trk}

    def other_trk(distance):
        return {"blk": blk, "trk": lax.rem(trk + distance, shares)}

    peers = [other_blk(d) for d in range(1, owners)] + [other_trk(d) for d in range(1, shares)]
    barrier = pltpu.get_barrier_semaphore()
    for peer in peers:
        pl.semaphore_signal(barrier, inc=1, device_id=peer, device_id_type=pl.DeviceIdType.MESH)

    def copy(source, target, send, recv, peer):
        return pltpu.make_async_remote_copy(
            src_ref=source,
            dst_ref=target,
            send_sem=send,
            recv_sem=recv,
            device_id=peer,
            device_id_type=pl.DeviceIdType.MESH,
        )

    started = []

    table[blk, :, 0:NB] = pattern_ref[...]
    pl.semaphore_wait(barrier, len(peers))
    sent = [
        copy(table.at[blk], table.at[blk], table_send.at[d - 1], table_recv.at[d - 1], other_blk(d))
        for d in range(1, owners)
    ]
    for one in sent:
        one.start()
    started += sent

    track_of = lax.broadcasted_iota(jnp.int32, (tracks, rows), 1) // SEG
    track_id = lax.broadcasted_iota(jnp.int32, (tracks, rows), 0)
    kept_rows = jnp.dot(
        jnp.broadcast_to(kept_ref[...].astype(jnp.float32), (WIDE, tracks)).astype(jnp.bfloat16),
        (track_of == track_id).astype(jnp.float32).astype(jnp.bfloat16),
        preferred_element_type=jnp.float32,
    )[0:1]
    scaling = kept_rows * invsig_ref[...].astype(jnp.float32)
    scaled = (scaling * derivs_ref[...].astype(jnp.float32)).astype(jnp.bfloat16).astype(jnp.float32)
    weighted = (scaling * resid_ref[...].astype(jnp.float32)).astype(jnp.bfloat16).astype(jnp.float32)
    none = jnp.zeros((WIDE - PAR, rows), jnp.float32)
    derivs = jnp.concatenate(
        [
            jnp.concatenate([scaled[0:PAR], none], axis=0),
            jnp.concatenate([scaled[PAR : 2 * PAR], none], axis=0),
        ],
        axis=1,
    )
    first_block = block_ref[...]
    first_module = first_block * MODS + hits_ref[0:1]
    module_ids = lax.broadcasted_iota(jnp.int32, (modules, rows), 0)
    onehot[:, 0:rows] = (module_ids == first_module).astype(jnp.float32).astype(jnp.bfloat16)

    place_row = lax.broadcasted_iota(jnp.int32, (order_size, LANES), 0) // PAR
    place_lane = lax.broadcasted_iota(jnp.int32, (order_size, LANES), 1)
    half = lax.rem(blk, per_share)
    place = (place_lane == place_row + half * MODS).astype(jnp.float32).astype(jnp.bfloat16)
    component = lax.broadcasted_iota(jnp.int32, (WIDE, order_size), 0)
    parameter = lax.broadcasted_iota(jnp.int32, (WIDE, order_size), 1)
    own_entry = component == lax.rem(parameter, PAR)
    spread_prior = jnp.where(own_entry, prior_ref[...], 0.0)
    prior_parts = jnp.dot(three_parts(spread_prior), place, preferred_element_type=jnp.float32)
    own_prior = prior_parts[0:WIDE] + prior_parts[WIDE : 2 * WIDE] + prior_parts[2 * WIDE :]
    own_prior = jnp.where(trk == 0, own_prior, 0.0)
    own_share = blk // per_share
    prior = [jnp.where(own_share == j, own_prior, 0.0) for j in range(shares)]

    def in_order(vector_ref):
        parts = three_parts(vector_ref[own_share])
        laid = lax.dot_general(
            parts, place, (((1,), (1,)), ((), ())), preferred_element_type=jnp.float32
        )
        laid = laid[0:WIDE] + laid[WIDE : 2 * WIDE] + laid[2 * WIDE :]
        return jnp.sum(jnp.where(own_entry, laid, 0.0), axis=0, keepdims=True)

    for one in sent:
        one.wait_recv()
    patterns = table[...].reshape(owners, LANES).astype(jnp.float32)
    block_ids = lax.broadcasted_iota(jnp.int32, (owners, rows), 0)
    names = (block_ids == first_block).astype(jnp.float32)
    slot = slot_ref[...]
    second_block = jnp.zeros((1, rows), jnp.float32)
    for s in range(NB):
        value = jnp.sum(names * patterns[:, s : s + 1], axis=0, keepdims=True)
        second_block = jnp.where(slot == s, value, second_block)
    second_module = second_block.astype(jnp.int32) * MODS + hits_ref[1:2]
    onehot[:, rows : 2 * rows] = (module_ids == second_module).astype(jnp.float32).astype(jnp.bfloat16)

    def scatter(row_values):
        both = jnp.concatenate([row_values, row_values], axis=1)
        summed = lax.dot_general(
            two_parts(derivs * both),
            onehot[...],
            (((1,), (1,)), ((), ())),
            preferred_element_type=jnp.float32,
        )
        return summed[0:WIDE] + summed[WIDE : 2 * WIDE]

    def gather(vector):
        read = jnp.dot(two_parts(vector), onehot[...], preferred_element_type=jnp.float32)
        read = read[0:WIDE] + read[WIDE : 2 * WIDE]
        along = jnp.sum(derivs * read, axis=0, keepdims=True)
        return along[:, 0:rows] + along[:, rows : 2 * rows]

    def add_up(phase, terms):
        for j in range(shares):
            part[phase, j] = terms[j]
        sent = []
        for d in range(1, shares):
            sent.append(
                copy(
                    part.at[phase, lax.rem(trk + d, shares)],
                    landed.at[phase, d - 1],
                    part_send.at[phase, d - 1],
                    part_recv.at[phase, d - 1],
                    other_trk(d),
                )
            )
        for one in sent:
            one.start()
        own = part[phase, trk]
        for one in sent:
            one.wait_recv()
        started.extend(sent)
        for d in range(1, shares):
            own = own + landed[phase, d - 1]
        blocks[phase, blk] = own
        sent = []
        for d in range(1, owners):
            sent.append(
                copy(
                    blocks.at[phase, blk],
                    blocks.at[phase, blk],
                    block_send.at[phase, d - 1],
                    block_recv.at[phase, d - 1],
                    other_blk(d),
                )
            )
        for one in sent:
            one.start()
        for one in sent:
            one.wait_recv()
        started.extend(sent)
        summed = blocks[phase, 0]
        for k in range(1, owners):
            summed = summed + blocks[phase, k]
        full[phase, trk] = summed
        sent = []
        for d in range(1, shares):
            sent.append(
                copy(
                    full.at[phase, trk],
                    full.at[phase, trk],
                    full_send.at[phase, d - 1],
                    full_recv.at[phase, d - 1],
                    other_trk(d),
                )
            )
        for one in sent:
            one.start()
        for one in sent:
            one.wait_recv()
        started.extend(sent)
        return jnp.concatenate([full[phase, j] for j in range(shares)], axis=1)

    def pieces(vector):
        return [vector[:, j * LANES : (j + 1) * LANES] for j in range(shares)]

    gradient = add_up(0, pieces(scatter(weighted)))
    initial_norm = jnp.sqrt(total(gradient * gradient) + epsilon)
    current = gradient / initial_norm
    previous = jnp.zeros_like(gradient)
    beta_term = jnp.zeros((1, 1), jnp.float32)
    diag_terms, off_terms, basis_list = ([], [], [])
    for iteration in range(ITERS):
        terms = pieces(scatter(gather(current)))
        for j, values in enumerate(pieces(current)):
            terms[j] = terms[j] + prior[j] * values
        image_vec = add_up(iteration + 1, terms)
        alpha_term = total(current * image_vec)
        direction = image_vec - alpha_term * current - beta_term * previous
        beta_next = jnp.sqrt(total(direction * direction) + epsilon)
        diag_terms.append(alpha_term)
        off_terms.append(beta_next)
        basis_list.append(current)
        previous, current, beta_term = (current, direction / beta_next, beta_next)
    out_ref[1:2] = in_order(full.at[0])

    first, second = diag_terms
    below, last = off_terms
    corner = first * first + below * below
    side = first * below + below * second
    end = below * below + second * second + last * last
    root = jnp.sqrt(corner)
    lower = side / root
    tip = jnp.sqrt(end - lower * lower)
    forward = initial_norm * first / root
    forward_next = (initial_norm * below - lower * forward) / tip
    back_next = forward_next / tip
    back = (forward - lower * back_next) / root
    result = back * basis_list[0] + back_next * basis_list[1]
    for j, values in enumerate(pieces(result)):
        part[PHASES, j] = values
    out_ref[0:1] = in_order(part.at[PHASES])
    for one in started:
        one.wait_send()


def on_device(
    row_block,
    row_hits,
    row_slot,
    track_kept,
    row_derivs,
    row_resid,
    row_invsig,
    pattern,
    prior,
    owners,
    shares,
):
    args = (
        row_block, row_hits, row_slot, track_kept, row_derivs, row_resid, row_invsig, pattern, prior
    )
    if owners * MODS != shares * LANES:
        return on_device_large(*args)
    rows = row_resid.shape[0]
    dma = pltpu.SemaphoreType.DMA
    tile = (WIDE, LANES)
    out = pl.pallas_call(
        functools.partial(kernel, owners, shares),
        out_shape=jax.ShapeDtypeStruct((2, MODS * PAR), jnp.float32),
        in_specs=[pl.BlockSpec(memory_space=pltpu.VMEM)] * 9,
        out_specs=pl.BlockSpec(memory_space=pltpu.VMEM),
        scratch_shapes=[
            pltpu.VMEM((owners * MODS, 2 * rows), jnp.bfloat16),
            pltpu.VMEM((owners, 1, LANES), jnp.int32),
            pltpu.VMEM((PHASES + 1, shares) + tile, jnp.float32),
            pltpu.VMEM((PHASES, shares - 1) + tile, jnp.float32),
            pltpu.VMEM((PHASES, owners) + tile, jnp.float32),
            pltpu.VMEM((PHASES + 1, shares) + tile, jnp.float32),
            dma((owners - 1,)),
            dma((owners - 1,)),
            dma((PHASES, shares - 1)),
            dma((PHASES, shares - 1)),
            dma((PHASES, owners - 1)),
            dma((PHASES, owners - 1)),
            dma((PHASES, shares - 1)),
            dma((PHASES, shares - 1)),
        ],
        compiler_params=pltpu.CompilerParams(
            collective_id=0, has_side_effects=True, vmem_limit_bytes=16 * 1024 * 1024
        ),
    )(
        row_block.reshape(1, rows),
        row_hits,
        row_slot.reshape(1, rows),
        track_kept.reshape(1, -1),
        row_derivs,
        row_resid.reshape(1, rows),
        row_invsig.reshape(1, rows),
        pattern,
        prior,
    )
    return out[0:1], out[1:2]


def solution(mesh):
    return jax.shard_map(
        functools.partial(on_device, owners=mesh.shape["blk"], shares=mesh.shape["trk"]),
        mesh=mesh,
        in_specs=(
            P(("blk", "trk"), None),
            P(None, ("blk", "trk")),
            P(("blk", "trk")),
            P(("blk", "trk")),
            P(None, ("blk", "trk")),
            P(("blk", "trk")),
            P(("blk", "trk")),
            P("blk", None),
            P("blk", None),
        ),
        out_specs=(P("blk", None), P("blk", None)),
        check_vma=False,
    )
```

```python
import functools

import jax
import jax.numpy as jnp
from jax import lax
from jax.experimental import pallas as pl
from jax.experimental.pallas import tpu as pltpu
from jax.sharding import PartitionSpec as P

MODS = 64
PAR = 6
NB = 5
SEG = 8
ITERS = 2


epsilon = 1e-06


def passed_along(block, axis, distance):
    devices = range(lax.axis_size(axis))
    route = [((i - distance) % len(devices), i) for i in devices]
    return lax.ppermute(block, axis, route)


def project(initial_norm, diag_terms, off_terms, basis_list):
    size_count = len(diag_terms)
    zero_value = diag_terms[0] * 0.0
    rows_list = []
    for row_index in range(size_count + 1):
        entries = []
        for column in range(size_count):
            if row_index == column:
                entries.append(diag_terms[column])
            elif row_index == column + 1:
                entries.append(off_terms[column])
            elif column == row_index + 1:
                entries.append(off_terms[row_index])
            else:
                entries.append(zero_value)
        rows_list.append(jnp.stack(entries))
    tridiagonal = jnp.stack(rows_list)
    gram_matrix = jnp.dot(tridiagonal.T, tridiagonal, precision=lax.Precision.HIGHEST)
    target = initial_norm * tridiagonal[0]
    factor = jnp.linalg.cholesky(gram_matrix)
    forward = []
    for row_index in range(size_count):
        partial_sum = target[row_index]
        for column in range(row_index):
            partial_sum = partial_sum - factor[row_index, column] * forward[column]
        forward.append(partial_sum / factor[row_index, row_index])
    backward = [zero_value] * size_count
    for row_index in reversed(range(size_count)):
        partial_sum = forward[row_index]
        for column in range(row_index + 1, size_count):
            partial_sum = partial_sum - factor[column, row_index] * backward[column]
        backward[row_index] = partial_sum / factor[row_index, row_index]
    solution = backward[0] * basis_list[0]
    row_index = 1
    solution = solution + backward[row_index] * basis_list[row_index]
    return solution


def contract(left_rows, right_rows):
    return lax.dot_general(
        left_rows, right_rows, (((0,), (0,)), ((), ())), preferred_element_type=jnp.float32
    )


def on_device_large(
    row_block, row_hits, row_slot, track_kept, row_derivs, row_resid, row_invsig, pattern, prior
):
    row_count = row_resid.shape[0]
    owners = lax.axis_size("blk")
    capacity = 2 * row_count // owners
    order_size = MODS * PAR
    kept_rows = jnp.repeat(track_kept, SEG).astype(jnp.float32)
    scaling = kept_rows * row_invsig.astype(jnp.float32)
    scaled = (scaling[None, :] * row_derivs.astype(jnp.float32)).astype(jnp.bfloat16)
    weighted = (scaling * row_resid.astype(jnp.float32)).astype(jnp.bfloat16)
    destination = row_block[:, 0]
    member = (destination[:, None] == jnp.arange(owners, dtype=jnp.int32)[None, :]).astype(
        jnp.bfloat16
    )
    row_ids = jnp.arange(row_count, dtype=jnp.int32)
    earlier = (row_ids[:, None] > row_ids[None, :]).astype(jnp.bfloat16)
    before = jnp.dot(earlier, member, preferred_element_type=jnp.float32)
    rank_within = jnp.sum(before * member.astype(jnp.float32), axis=1).astype(jnp.int32)
    slot_place = destination * capacity + rank_within
    labels = jnp.stack([row_hits[0], row_hits[1], row_slot]).astype(jnp.bfloat16)
    record = jnp.concatenate([scaled, weighted[None, :], labels], axis=0)
    outgoing = (
        jnp.zeros((record.shape[0], owners * capacity), jnp.bfloat16).at[:, slot_place].set(record)
    )
    incoming = lax.all_to_all(outgoing, "blk", split_axis=1, concat_axis=1, tiled=True)
    column_ids = jnp.arange(order_size, dtype=jnp.int32)
    column_module = column_ids // PAR
    column_param = column_ids % PAR

    def expand(values, module_ids):
        spread = jnp.zeros((values.shape[1], order_size), jnp.bfloat16)
        for component in range(PAR):
            spread = jnp.where(
                column_param[None, :] == component, values[component][:, None], spread
            )
        return jnp.where(
            module_ids[:, None] == column_module[None, :], spread, jnp.zeros_like(spread)
        )

    first_module = incoming[2 * PAR + 1].astype(jnp.int32)
    second_module = incoming[2 * PAR + 2].astype(jnp.int32)
    slot_in = incoming[2 * PAR + 3].astype(jnp.int32)
    resid_in = incoming[2 * PAR]
    first_rows = expand(incoming[0:PAR], first_module)
    second_rows = expand(incoming[PAR : 2 * PAR], second_module)
    own_block = contract(first_rows, first_rows)
    grad_own = jnp.dot(resid_in, first_rows, preferred_element_type=jnp.float32)
    cross_list, partner_list, grad_list = ([], [], [])
    for slot_id in range(NB):
        masked = jnp.where((slot_in == slot_id)[:, None], second_rows, jnp.zeros_like(second_rows))
        cross_list.append(contract(first_rows, masked))
        partner_list.append(contract(masked, masked))
        grad_list.append(jnp.dot(resid_in, masked, preferred_element_type=jnp.float32))
    cross_blocks = jnp.stack(cross_list)
    partner_blocks = jnp.stack(partner_list)
    grad_partner = jnp.stack(grad_list)
    position = lax.axis_index("blk")
    neighbours = pattern[0]
    offset = (neighbours - position) % owners
    offset = jnp.where(offset > owners // 2, offset - owners, offset)

    def deliver(own_term, partner_terms):
        local_sum = own_term + jnp.sum(
            jnp.where((offset == 0)[:, None], partner_terms, 0.0), axis=0, keepdims=True
        )
        for shift_by in (-2, -1, 1, 2):
            sending = jnp.sum(
                jnp.where((offset == shift_by)[:, None], partner_terms, 0.0), axis=0, keepdims=True
            )
            local_sum = local_sum + passed_along(sending, "blk", shift_by)
        return lax.psum(local_sum, "trk")

    gradient = deliver(grad_own[None, :], grad_partner)
    initial_norm = jnp.sqrt(lax.psum(jnp.sum(gradient * gradient), "blk") + epsilon)
    current = gradient / initial_norm
    previous = jnp.zeros_like(gradient)
    beta_term = jnp.zeros((), jnp.float32)
    diag_terms, off_terms, basis_list = ([], [], [])
    for iteration in range(ITERS):
        result = jnp.where((offset == 0)[:, None], current, 0.0)
        for fetch_shift_by in (-2, -1, 1, 2):
            arrived = passed_along(current, "blk", -fetch_shift_by)
            result = result + jnp.where((offset == fetch_shift_by)[:, None], arrived, 0.0)
        operate_own_term = jnp.dot(own_block, current[0], precision=lax.Precision.HIGHEST)
        operate_own_term = operate_own_term + jnp.einsum(
            "kij,kj->i", cross_blocks, result, precision=lax.Precision.HIGHEST
        )
        operate_partner_terms = jnp.einsum(
            "kij,i->kj", cross_blocks, current[0], precision=lax.Precision.HIGHEST
        )
        operate_partner_terms = operate_partner_terms + jnp.einsum(
            "kij,kj->ki", partner_blocks, result, precision=lax.Precision.HIGHEST
        )
        image_vec = prior * current + deliver(operate_own_term[None, :], operate_partner_terms)
        alpha_term = lax.psum(jnp.sum(current * image_vec), "blk")
        direction = image_vec - alpha_term * current - beta_term * previous
        beta_next = jnp.sqrt(lax.psum(jnp.sum(direction * direction), "blk") + epsilon)
        diag_terms.append(alpha_term)
        off_terms.append(beta_next)
        basis_list.append(current)
        previous, current, beta_term = (current, direction / beta_next, beta_next)
    solution = project(initial_norm, diag_terms, off_terms, basis_list)
    return (solution, gradient)


LANES = 128
WIDE = 8
PHASES = ITERS + 1


def two_parts(value):
    high = value.astype(jnp.bfloat16)
    low = (value - high.astype(jnp.float32)).astype(jnp.bfloat16)
    return jnp.concatenate([high, low], axis=0)


def three_parts(value):
    high = value.astype(jnp.bfloat16).astype(jnp.float32)
    rest = value - high
    middle = rest.astype(jnp.bfloat16).astype(jnp.float32)
    return jnp.concatenate([high, middle, rest - middle], axis=0).astype(jnp.bfloat16)


def total(value):
    return jnp.sum(jnp.sum(value, axis=0, keepdims=True), axis=1, keepdims=True)


def kernel(
    owners,
    shares,
    block_ref,
    hits_ref,
    slot_ref,
    kept_ref,
    derivs_ref,
    resid_ref,
    invsig_ref,
    pattern_ref,
    prior_ref,
    out_ref,
    block_in,
    hits_in,
    slot_in,
    kept_in,
    derivs_in,
    resid_in,
    invsig_in,
    pattern_in,
    prior_in,
    input_sem,
    onehot,
    table,
    part,
    landed,
    blocks,
    full,
    table_send,
    table_recv,
    part_send,
    part_recv,
    block_send,
    block_recv,
    full_send,
    full_recv,
):
    blk, trk = lax.axis_index("blk"), lax.axis_index("trk")
    rows = block_ref.shape[1]
    tracks = kept_ref.shape[1]
    outside = (
        pattern_ref, kept_ref, invsig_ref, derivs_ref, resid_ref, block_ref, hits_ref, slot_ref, prior_ref
    )
    inside = (
        pattern_in, kept_in, invsig_in, derivs_in, resid_in, block_in, hits_in, slot_in, prior_in
    )
    fetches = [
        pltpu.make_async_copy(source, target, input_sem.at[i])
        for i, (source, target) in enumerate(zip(outside, inside))
    ]
    for one in fetches:
        one.start()
    modules = owners * MODS
    order_size = MODS * PAR
    per_share = LANES // MODS

    def other_blk(distance):
        return {"blk": lax.rem(blk + distance, owners), "trk": trk}

    pairs, width = shares // 2, shares // 2
    pair, half = trk // 2, lax.rem(trk, 2)
    sibling = {"blk": blk, "trk": pair * 2 + 1 - half}

    def other_pair(c, j):
        return {"blk": lax.rem(blk + c, owners), "trk": lax.rem(pair + j, pairs) * 2 + half}

    steps = [(c, j) for c in range(owners) for j in range(pairs) if c or j]
    steps.sort(key=lambda step: (abs(step[0] - owners // 2), -step[1]))
    peers = [sibling] + [other_pair(c, j) for c, j in steps]
    barrier = pltpu.get_barrier_semaphore()
    for peer in peers:
        pl.semaphore_signal(barrier, inc=1, device_id=peer, device_id_type=pl.DeviceIdType.MESH)

    def copy(source, target, send, recv, peer):
        return pltpu.make_async_remote_copy(
            src_ref=source,
            dst_ref=target,
            send_sem=send,
            recv_sem=recv,
            device_id=peer,
            device_id_type=pl.DeviceIdType.MESH,
        )

    started = []
    fetches[0].wait()

    table[blk, :, 0:NB] = pattern_in[...]
    pl.semaphore_wait(barrier, len(peers))
    sent = [
        copy(table.at[blk], table.at[blk], table_send.at[d - 1], table_recv.at[d - 1], other_blk(d))
        for d in range(1, owners)
    ]
    for one in sent:
        one.start()
    started += sent

    for one in fetches[1:]:
        one.wait()

    track_of = lax.broadcasted_iota(jnp.int32, (tracks, rows), 1) // SEG
    track_id = lax.broadcasted_iota(jnp.int32, (tracks, rows), 0)
    kept_rows = jnp.dot(
        jnp.broadcast_to(kept_in[...].astype(jnp.float32), (WIDE, tracks)).astype(jnp.bfloat16),
        (track_of == track_id).astype(jnp.float32).astype(jnp.bfloat16),
        preferred_element_type=jnp.float32,
    )[0:1]
    scaling = kept_rows * invsig_in[...].reshape(1, rows).astype(jnp.float32)
    scaled = (scaling * derivs_in[...].astype(jnp.float32)).astype(jnp.bfloat16).astype(jnp.float32)
    weighted = (scaling * resid_in[...].reshape(1, rows).astype(jnp.float32)).astype(jnp.bfloat16).astype(jnp.float32)
    none = jnp.zeros((WIDE - PAR, rows), jnp.float32)
    derivs = jnp.concatenate(
        [
            jnp.concatenate([scaled[0:PAR], none], axis=0),
            jnp.concatenate([scaled[PAR : 2 * PAR], none], axis=0),
        ],
        axis=1,
    )
    first_block = block_in[...]
    first_module = first_block * MODS + hits_in[0:1]
    module_ids = lax.broadcasted_iota(jnp.int32, (modules, rows), 0)
    onehot[:, 0:rows] = (module_ids == first_module).astype(jnp.float32).astype(jnp.bfloat16)

    place_row = lax.broadcasted_iota(jnp.int32, (order_size, LANES), 0) // PAR
    place_lane = lax.broadcasted_iota(jnp.int32, (order_size, LANES), 1)
    lane_half = lax.rem(blk, per_share)
    place = (place_lane == place_row + lane_half * MODS).astype(jnp.float32).astype(jnp.bfloat16)
    component = lax.broadcasted_iota(jnp.int32, (WIDE, order_size), 0)
    parameter = lax.broadcasted_iota(jnp.int32, (WIDE, order_size), 1)
    own_entry = component == lax.rem(parameter, PAR)
    spread_prior = jnp.where(own_entry, prior_in[...], 0.0)
    prior_parts = jnp.dot(three_parts(spread_prior), place, preferred_element_type=jnp.float32)
    own_prior = prior_parts[0:WIDE] + prior_parts[WIDE : 2 * WIDE] + prior_parts[2 * WIDE :]
    own_prior = jnp.where(trk == 0, own_prior, 0.0)
    own_share = blk // per_share
    prior = [jnp.where(own_share == j, own_prior, 0.0) for j in range(shares)]

    def in_order(vector):
        own = jnp.zeros((WIDE, LANES), jnp.float32)
        for j in range(shares):
            own = jnp.where(own_share == j, vector[:, j * LANES : (j + 1) * LANES], own)
        parts = three_parts(own)
        laid = lax.dot_general(
            parts, place, (((1,), (1,)), ((), ())), preferred_element_type=jnp.float32
        )
        laid = laid[0:WIDE] + laid[WIDE : 2 * WIDE] + laid[2 * WIDE :]
        return jnp.sum(jnp.where(own_entry, laid, 0.0), axis=0, keepdims=True)

    for one in sent:
        one.wait_recv()
    patterns = table[...].reshape(owners, LANES).astype(jnp.float32)
    block_ids = lax.broadcasted_iota(jnp.int32, (owners, rows), 0)
    names = (block_ids == first_block).astype(jnp.float32)
    slot = slot_in[...]
    second_block = jnp.zeros((1, rows), jnp.float32)
    for s in range(NB):
        value = jnp.sum(names * patterns[:, s : s + 1], axis=0, keepdims=True)
        second_block = jnp.where(slot == s, value, second_block)
    second_module = second_block.astype(jnp.int32) * MODS + hits_in[1:2]
    onehot[:, rows : 2 * rows] = (module_ids == second_module).astype(jnp.float32).astype(jnp.bfloat16)

    def scatter(row_values):
        both = jnp.concatenate([row_values, row_values], axis=1)
        summed = lax.dot_general(
            two_parts(derivs * both),
            onehot[...],
            (((1,), (1,)), ((), ())),
            preferred_element_type=jnp.float32,
        )
        return summed[0:WIDE] + summed[WIDE : 2 * WIDE]

    def gather(vector):
        read = jnp.dot(two_parts(vector), onehot[...], preferred_element_type=jnp.float32)
        read = read[0:WIDE] + read[WIDE : 2 * WIDE]
        along = jnp.sum(derivs * read, axis=0, keepdims=True)
        return along[:, 0:rows] + along[:, rows : 2 * rows]

    def add_up(phase, terms):
        for j in range(shares):
            part[phase, j // width, j % width] = terms[j]
        swap = copy(
            part.at[phase, 1 - half, :, 0:PAR],
            landed.at[phase, :, 0:PAR],
            part_send.at[phase],
            part_recv.at[phase],
            sibling,
        )
        swap.start()
        own = part[phase, half]
        swap.wait_recv()
        blocks[phase, blk, pair] = own + landed[phase]
        sent = [
            copy(
                blocks.at[phase, blk, pair, :, 0:PAR],
                blocks.at[phase, blk, pair, :, 0:PAR],
                block_send.at[phase, c, j],
                block_recv.at[phase, c, j],
                other_pair(c, j),
            )
            for c, j in steps
        ]
        for one in sent:
            one.start()
        for one in sent:
            one.wait_recv()
        summed = blocks[phase, 0, 0, :, 0:PAR]
        for k in range(1, owners * pairs):
            summed = summed + blocks[phase, k // pairs, k % pairs, :, 0:PAR]
        full[phase, half, :, 0:PAR] = summed
        join = copy(
            full.at[phase, half, :, 0:PAR],
            full.at[phase, half, :, 0:PAR],
            full_send.at[phase],
            full_recv.at[phase],
            sibling,
        )
        join.start()
        join.wait_recv()
        started.extend([swap, join] + sent)
        read = [full[phase, j // width, j % width, 0:PAR] for j in range(shares)]
        empty = jnp.zeros((WIDE - PAR, shares * LANES), jnp.float32)
        return jnp.concatenate([jnp.concatenate(read, axis=1), empty], axis=0)

    def pieces(vector):
        return [vector[:, j * LANES : (j + 1) * LANES] for j in range(shares)]

    gradient = add_up(0, pieces(scatter(weighted)))
    initial_norm = jnp.sqrt(total(gradient * gradient) + epsilon)
    current = gradient / initial_norm
    previous = jnp.zeros_like(gradient)
    beta_term = jnp.zeros((1, 1), jnp.float32)
    diag_terms, off_terms, basis_list = ([], [], [])
    for iteration in range(ITERS):
        terms = pieces(scatter(gather(current)))
        for j, values in enumerate(pieces(current)):
            terms[j] = terms[j] + prior[j] * values
        image_vec = add_up(iteration + 1, terms)
        alpha_term = total(current * image_vec)
        direction = image_vec - alpha_term * current - beta_term * previous
        beta_next = jnp.sqrt(total(direction * direction) + epsilon)
        diag_terms.append(alpha_term)
        off_terms.append(beta_next)
        basis_list.append(current)
        previous, current, beta_term = (current, direction / beta_next, beta_next)
    out_ref[1:2] = in_order(gradient)

    first, second = diag_terms
    below, last = off_terms
    corner = first * first + below * below
    side = first * below + below * second
    end = below * below + second * second + last * last
    root = jnp.sqrt(corner)
    lower = side / root
    tip = jnp.sqrt(end - lower * lower)
    forward = initial_norm * first / root
    forward_next = (initial_norm * below - lower * forward) / tip
    back_next = forward_next / tip
    back = (forward - lower * back_next) / root
    result = back * basis_list[0] + back_next * basis_list[1]
    out_ref[0:1] = in_order(result)
    for one in started:
        one.wait_send()


def on_device(
    row_block,
    row_hits,
    row_slot,
    track_kept,
    row_derivs,
    row_resid,
    row_invsig,
    pattern,
    prior,
    owners,
    shares,
):
    args = (
        row_block, row_hits, row_slot, track_kept, row_derivs, row_resid, row_invsig, pattern, prior
    )
    if owners * MODS != shares * LANES or shares % 2:
        return on_device_large(*args)
    rows = row_resid.shape[0]
    dma = pltpu.SemaphoreType.DMA
    tile = (WIDE, LANES)
    width = shares // 2
    out = pl.pallas_call(
        functools.partial(kernel, owners, shares),
        out_shape=jax.ShapeDtypeStruct((2, MODS * PAR), jnp.float32),
        in_specs=[pl.BlockSpec(memory_space=pltpu.HBM)] * 9,
        out_specs=pl.BlockSpec(memory_space=pltpu.VMEM),
        scratch_shapes=[
            pltpu.VMEM((1, rows), jnp.int32),
            pltpu.VMEM((2, rows), jnp.int32),
            pltpu.VMEM((1, rows), jnp.int32),
            pltpu.VMEM((1, track_kept.shape[0]), jnp.int32),
            pltpu.VMEM((2 * PAR, rows), jnp.bfloat16),
            pltpu.VMEM((rows,), jnp.bfloat16),
            pltpu.VMEM((rows,), jnp.bfloat16),
            pltpu.VMEM((1, NB), jnp.int32),
            pltpu.VMEM((1, MODS * PAR), jnp.float32),
            dma((9,)),
            pltpu.VMEM((owners * MODS, 2 * rows), jnp.bfloat16),
            pltpu.VMEM((owners, 1, LANES), jnp.int32),
            pltpu.VMEM((PHASES, 2, width) + tile, jnp.float32),
            pltpu.VMEM((PHASES, width) + tile, jnp.float32),
            pltpu.VMEM((PHASES, owners, shares // 2, width) + tile, jnp.float32),
            pltpu.VMEM((PHASES, 2, width) + tile, jnp.float32),
            dma((owners - 1,)),
            dma((owners - 1,)),
            dma((PHASES,)),
            dma((PHASES,)),
            dma((PHASES, owners, shares // 2)),
            dma((PHASES, owners, shares // 2)),
            dma((PHASES,)),
            dma((PHASES,)),
        ],
        compiler_params=pltpu.CompilerParams(
            collective_id=0, has_side_effects=True, vmem_limit_bytes=60 * 1024 * 1024
        ),
    )(
        row_block.reshape(1, rows),
        row_hits,
        row_slot.reshape(1, rows),
        track_kept.reshape(1, -1),
        row_derivs,
        row_resid,
        row_invsig,
        pattern,
        prior,
    )
    return out[0:1], out[1:2]


def solution(mesh):
    return jax.shard_map(
        functools.partial(on_device, owners=mesh.shape["blk"], shares=mesh.shape["trk"]),
        mesh=mesh,
        in_specs=(
            P(("blk", "trk"), None),
            P(None, ("blk", "trk")),
            P(("blk", "trk")),
            P(("blk", "trk")),
            P(None, ("blk", "trk")),
            P(("blk", "trk")),
            P(("blk", "trk")),
            P("blk", None),
            P("blk", None),
        ),
        out_specs=(P("blk", None), P("blk", None)),
        check_vma=False,
    )
```

```python
import functools

import jax
import jax.numpy as jnp
from jax import lax
from jax.experimental import pallas as pl
from jax.experimental.pallas import tpu as pltpu
from jax.sharding import PartitionSpec as P

MODS = 64
PAR = 6
NB = 5
SEG = 8
ITERS = 2


epsilon = 1e-06


def passed_along(block, axis, distance):
    devices = range(lax.axis_size(axis))
    route = [((i - distance) % len(devices), i) for i in devices]
    return lax.ppermute(block, axis, route)


def project(initial_norm, diag_terms, off_terms, basis_list):
    size_count = len(diag_terms)
    zero_value = diag_terms[0] * 0.0
    rows_list = []
    for row_index in range(size_count + 1):
        entries = []
        for column in range(size_count):
            if row_index == column:
                entries.append(diag_terms[column])
            elif row_index == column + 1:
                entries.append(off_terms[column])
            elif column == row_index + 1:
                entries.append(off_terms[row_index])
            else:
                entries.append(zero_value)
        rows_list.append(jnp.stack(entries))
    tridiagonal = jnp.stack(rows_list)
    gram_matrix = jnp.dot(tridiagonal.T, tridiagonal, precision=lax.Precision.HIGHEST)
    target = initial_norm * tridiagonal[0]
    factor = jnp.linalg.cholesky(gram_matrix)
    forward = []
    for row_index in range(size_count):
        partial_sum = target[row_index]
        for column in range(row_index):
            partial_sum = partial_sum - factor[row_index, column] * forward[column]
        forward.append(partial_sum / factor[row_index, row_index])
    backward = [zero_value] * size_count
    for row_index in reversed(range(size_count)):
        partial_sum = forward[row_index]
        for column in range(row_index + 1, size_count):
            partial_sum = partial_sum - factor[column, row_index] * backward[column]
        backward[row_index] = partial_sum / factor[row_index, row_index]
    solution = backward[0] * basis_list[0]
    row_index = 1
    solution = solution + backward[row_index] * basis_list[row_index]
    return solution


def contract(left_rows, right_rows):
    return lax.dot_general(
        left_rows, right_rows, (((0,), (0,)), ((), ())), preferred_element_type=jnp.float32
    )


def on_device_large(
    row_block, row_hits, row_slot, track_kept, row_derivs, row_resid, row_invsig, pattern, prior
):
    row_count = row_resid.shape[0]
    owners = lax.axis_size("blk")
    capacity = 2 * row_count // owners
    order_size = MODS * PAR
    kept_rows = jnp.repeat(track_kept, SEG).astype(jnp.float32)
    scaling = kept_rows * row_invsig.astype(jnp.float32)
    scaled = (scaling[None, :] * row_derivs.astype(jnp.float32)).astype(jnp.bfloat16)
    weighted = (scaling * row_resid.astype(jnp.float32)).astype(jnp.bfloat16)
    destination = row_block[:, 0]
    member = (destination[:, None] == jnp.arange(owners, dtype=jnp.int32)[None, :]).astype(
        jnp.bfloat16
    )
    row_ids = jnp.arange(row_count, dtype=jnp.int32)
    earlier = (row_ids[:, None] > row_ids[None, :]).astype(jnp.bfloat16)
    before = jnp.dot(earlier, member, preferred_element_type=jnp.float32)
    rank_within = jnp.sum(before * member.astype(jnp.float32), axis=1).astype(jnp.int32)
    slot_place = destination * capacity + rank_within
    labels = jnp.stack([row_hits[0], row_hits[1], row_slot]).astype(jnp.bfloat16)
    record = jnp.concatenate([scaled, weighted[None, :], labels], axis=0)
    outgoing = (
        jnp.zeros((record.shape[0], owners * capacity), jnp.bfloat16).at[:, slot_place].set(record)
    )
    incoming = lax.all_to_all(outgoing, "blk", split_axis=1, concat_axis=1, tiled=True)
    column_ids = jnp.arange(order_size, dtype=jnp.int32)
    column_module = column_ids // PAR
    column_param = column_ids % PAR

    def expand(values, module_ids):
        spread = jnp.zeros((values.shape[1], order_size), jnp.bfloat16)
        for component in range(PAR):
            spread = jnp.where(
                column_param[None, :] == component, values[component][:, None], spread
            )
        return jnp.where(
            module_ids[:, None] == column_module[None, :], spread, jnp.zeros_like(spread)
        )

    first_module = incoming[2 * PAR + 1].astype(jnp.int32)
    second_module = incoming[2 * PAR + 2].astype(jnp.int32)
    slot_in = incoming[2 * PAR + 3].astype(jnp.int32)
    resid_in = incoming[2 * PAR]
    first_rows = expand(incoming[0:PAR], first_module)
    second_rows = expand(incoming[PAR : 2 * PAR], second_module)
    own_block = contract(first_rows, first_rows)
    grad_own = jnp.dot(resid_in, first_rows, preferred_element_type=jnp.float32)
    cross_list, partner_list, grad_list = ([], [], [])
    for slot_id in range(NB):
        masked = jnp.where((slot_in == slot_id)[:, None], second_rows, jnp.zeros_like(second_rows))
        cross_list.append(contract(first_rows, masked))
        partner_list.append(contract(masked, masked))
        grad_list.append(jnp.dot(resid_in, masked, preferred_element_type=jnp.float32))
    cross_blocks = jnp.stack(cross_list)
    partner_blocks = jnp.stack(partner_list)
    grad_partner = jnp.stack(grad_list)
    position = lax.axis_index("blk")
    neighbours = pattern[0]
    offset = (neighbours - position) % owners
    offset = jnp.where(offset > owners // 2, offset - owners, offset)

    def deliver(own_term, partner_terms):
        local_sum = own_term + jnp.sum(
            jnp.where((offset == 0)[:, None], partner_terms, 0.0), axis=0, keepdims=True
        )
        for shift_by in (-2, -1, 1, 2):
            sending = jnp.sum(
                jnp.where((offset == shift_by)[:, None], partner_terms, 0.0), axis=0, keepdims=True
            )
            local_sum = local_sum + passed_along(sending, "blk", shift_by)
        return lax.psum(local_sum, "trk")

    gradient = deliver(grad_own[None, :], grad_partner)
    initial_norm = jnp.sqrt(lax.psum(jnp.sum(gradient * gradient), "blk") + epsilon)
    current = gradient / initial_norm
    previous = jnp.zeros_like(gradient)
    beta_term = jnp.zeros((), jnp.float32)
    diag_terms, off_terms, basis_list = ([], [], [])
    for iteration in range(ITERS):
        result = jnp.where((offset == 0)[:, None], current, 0.0)
        for fetch_shift_by in (-2, -1, 1, 2):
            arrived = passed_along(current, "blk", -fetch_shift_by)
            result = result + jnp.where((offset == fetch_shift_by)[:, None], arrived, 0.0)
        operate_own_term = jnp.dot(own_block, current[0], precision=lax.Precision.HIGHEST)
        operate_own_term = operate_own_term + jnp.einsum(
            "kij,kj->i", cross_blocks, result, precision=lax.Precision.HIGHEST
        )
        operate_partner_terms = jnp.einsum(
            "kij,i->kj", cross_blocks, current[0], precision=lax.Precision.HIGHEST
        )
        operate_partner_terms = operate_partner_terms + jnp.einsum(
            "kij,kj->ki", partner_blocks, result, precision=lax.Precision.HIGHEST
        )
        image_vec = prior * current + deliver(operate_own_term[None, :], operate_partner_terms)
        alpha_term = lax.psum(jnp.sum(current * image_vec), "blk")
        direction = image_vec - alpha_term * current - beta_term * previous
        beta_next = jnp.sqrt(lax.psum(jnp.sum(direction * direction), "blk") + epsilon)
        diag_terms.append(alpha_term)
        off_terms.append(beta_next)
        basis_list.append(current)
        previous, current, beta_term = (current, direction / beta_next, beta_next)
    solution = project(initial_norm, diag_terms, off_terms, basis_list)
    return (solution, gradient)


LANES = 128
WIDE = 8
PHASES = ITERS + 1


def two_parts(value):
    high = value.astype(jnp.bfloat16)
    low = (value - high.astype(jnp.float32)).astype(jnp.bfloat16)
    return jnp.concatenate([high, low], axis=0)


def three_parts(value):
    high = value.astype(jnp.bfloat16).astype(jnp.float32)
    rest = value - high
    middle = rest.astype(jnp.bfloat16).astype(jnp.float32)
    return jnp.concatenate([high, middle, rest - middle], axis=0).astype(jnp.bfloat16)


def total(value):
    return jnp.sum(jnp.sum(value, axis=0, keepdims=True), axis=1, keepdims=True)


def kernel(
    owners,
    shares,
    block_ref,
    hits_ref,
    slot_ref,
    kept_ref,
    derivs_ref,
    resid_ref,
    invsig_ref,
    pattern_ref,
    prior_ref,
    out_ref,
    block_in,
    hits_in,
    slot_in,
    kept_in,
    derivs_in,
    resid_in,
    invsig_in,
    pattern_in,
    prior_in,
    input_sem,
    onehot,
    table,
    part,
    landed,
    blocks,
    full,
    table_send,
    table_recv,
    part_send,
    part_recv,
    block_send,
    block_recv,
    full_send,
    full_recv,
):
    blk, trk = lax.axis_index("blk"), lax.axis_index("trk")
    rows = block_ref.shape[1]
    tracks = kept_ref.shape[1]
    outside = (
        pattern_ref, kept_ref, invsig_ref, derivs_ref, resid_ref, block_ref, hits_ref, slot_ref, prior_ref
    )
    inside = (
        pattern_in, kept_in, invsig_in, derivs_in, resid_in, block_in, hits_in, slot_in, prior_in
    )
    fetches = [
        pltpu.make_async_copy(source, target, input_sem.at[i])
        for i, (source, target) in enumerate(zip(outside, inside))
    ]
    for one in fetches:
        one.start()
    modules = owners * MODS
    order_size = MODS * PAR
    per_share = LANES // MODS

    def other_blk(distance):
        return {"blk": lax.rem(blk + distance, owners), "trk": trk}

    pairs, width = shares // 2, shares // 2
    pair, half = trk // 2, lax.rem(trk, 2)
    sibling = {"blk": blk, "trk": pair * 2 + 1 - half}

    def other_pair(c, j):
        return {"blk": lax.rem(blk + c, owners), "trk": lax.rem(pair + j, pairs) * 2 + half}

    steps = [(c, j) for c in range(owners) for j in range(pairs) if c or j]
    steps.sort(key=lambda step: (abs(step[0] - owners // 2), -step[1]))
    peers = [sibling] + [other_pair(c, j) for c, j in steps]
    barrier = pltpu.get_barrier_semaphore()
    for peer in peers:
        pl.semaphore_signal(barrier, inc=1, device_id=peer, device_id_type=pl.DeviceIdType.MESH)

    def copy(source, target, send, recv, peer):
        return pltpu.make_async_remote_copy(
            src_ref=source,
            dst_ref=target,
            send_sem=send,
            recv_sem=recv,
            device_id=peer,
            device_id_type=pl.DeviceIdType.MESH,
        )

    started = []
    fetches[0].wait()

    table[blk, :, 0:NB] = pattern_in[...]
    pl.semaphore_wait(barrier, len(peers))
    sent = [
        copy(table.at[blk], table.at[blk], table_send.at[d - 1], table_recv.at[d - 1], other_blk(d))
        for d in range(1, owners)
    ]
    for one in sent:
        one.start()
    started += sent

    for one in fetches[1:]:
        one.wait()

    track_of = lax.broadcasted_iota(jnp.int32, (tracks, rows), 1) // SEG
    track_id = lax.broadcasted_iota(jnp.int32, (tracks, rows), 0)
    kept_rows = jnp.dot(
        jnp.broadcast_to(kept_in[...].astype(jnp.float32), (WIDE, tracks)).astype(jnp.bfloat16),
        (track_of == track_id).astype(jnp.float32).astype(jnp.bfloat16),
        preferred_element_type=jnp.float32,
    )[0:1]
    scaling = kept_rows * invsig_in[...].reshape(1, rows).astype(jnp.float32)
    scaled = (scaling * derivs_in[...].astype(jnp.float32)).astype(jnp.bfloat16).astype(jnp.float32)
    weighted = (scaling * resid_in[...].reshape(1, rows).astype(jnp.float32)).astype(jnp.bfloat16).astype(jnp.float32)
    none = jnp.zeros((WIDE - PAR, rows), jnp.float32)
    derivs = jnp.concatenate(
        [
            jnp.concatenate([scaled[0:PAR], none], axis=0),
            jnp.concatenate([scaled[PAR : 2 * PAR], none], axis=0),
        ],
        axis=1,
    )
    first_block = block_in[...]
    first_module = first_block * MODS + hits_in[0:1]
    module_ids = lax.broadcasted_iota(jnp.int32, (modules, rows), 0)
    onehot[:, 0:rows] = (module_ids == first_module).astype(jnp.float32).astype(jnp.bfloat16)

    place_row = lax.broadcasted_iota(jnp.int32, (order_size, LANES), 0) // PAR
    place_lane = lax.broadcasted_iota(jnp.int32, (order_size, LANES), 1)
    lane_half = lax.rem(blk, per_share)
    place = (place_lane == place_row + lane_half * MODS).astype(jnp.float32).astype(jnp.bfloat16)
    component = lax.broadcasted_iota(jnp.int32, (WIDE, order_size), 0)
    parameter = lax.broadcasted_iota(jnp.int32, (WIDE, order_size), 1)
    own_entry = component == lax.rem(parameter, PAR)
    spread_prior = jnp.where(own_entry, prior_in[...], 0.0)
    prior_parts = jnp.dot(three_parts(spread_prior), place, preferred_element_type=jnp.float32)
    own_prior = prior_parts[0:WIDE] + prior_parts[WIDE : 2 * WIDE] + prior_parts[2 * WIDE :]
    own_prior = jnp.where(trk == 0, own_prior, 0.0)
    own_share = blk // per_share
    prior = [jnp.where(own_share == j, own_prior, 0.0) for j in range(shares)]

    def in_order(vector):
        own = jnp.zeros((WIDE, LANES), jnp.float32)
        for j in range(shares):
            own = jnp.where(own_share == j, vector[:, j * LANES : (j + 1) * LANES], own)
        parts = three_parts(own)
        laid = lax.dot_general(
            parts, place, (((1,), (1,)), ((), ())), preferred_element_type=jnp.float32
        )
        laid = laid[0:WIDE] + laid[WIDE : 2 * WIDE] + laid[2 * WIDE :]
        return jnp.sum(jnp.where(own_entry, laid, 0.0), axis=0, keepdims=True)

    for one in sent:
        one.wait_recv()
    patterns = table[...].reshape(owners, LANES).astype(jnp.float32)
    block_ids = lax.broadcasted_iota(jnp.int32, (owners, rows), 0)
    names = (block_ids == first_block).astype(jnp.float32)
    slot = slot_in[...]
    second_block = jnp.zeros((1, rows), jnp.float32)
    for s in range(NB):
        value = jnp.sum(names * patterns[:, s : s + 1], axis=0, keepdims=True)
        second_block = jnp.where(slot == s, value, second_block)
    second_module = second_block.astype(jnp.int32) * MODS + hits_in[1:2]
    onehot[:, rows : 2 * rows] = (module_ids == second_module).astype(jnp.float32).astype(jnp.bfloat16)

    def scatter(row_values):
        both = jnp.concatenate([row_values, row_values], axis=1)
        summed = lax.dot_general(
            two_parts(derivs * both),
            onehot[...],
            (((1,), (1,)), ((), ())),
            preferred_element_type=jnp.float32,
        )
        return summed[0:WIDE] + summed[WIDE : 2 * WIDE]

    def gather(vector):
        read = jnp.dot(two_parts(vector), onehot[...], preferred_element_type=jnp.float32)
        read = read[0:WIDE] + read[WIDE : 2 * WIDE]
        along = jnp.sum(derivs * read, axis=0, keepdims=True)
        return along[:, 0:rows] + along[:, rows : 2 * rows]

    def add_up(phase, terms, beside=None):
        for j in range(shares):
            part[phase, j // width, j % width] = terms[j]
        swap = copy(
            part.at[phase, 1 - half, :, 0:PAR],
            landed.at[phase, :, 0:PAR],
            part_send.at[phase],
            part_recv.at[phase],
            sibling,
        )
        swap.start()
        own = part[phase, half]
        swap.wait_recv()
        blocks[phase, blk, pair] = own + landed[phase]
        sent = [
            copy(
                blocks.at[phase, blk, pair, :, 0:PAR],
                blocks.at[phase, blk, pair, :, 0:PAR],
                block_send.at[phase, c, j],
                block_recv.at[phase, c, j],
                other_pair(c, j),
            )
            for c, j in steps
        ]
        for one in sent:
            one.start()
        if beside is not None:
            beside()
        for one in sent:
            one.wait_recv()
        summed = blocks[phase, 0, 0, :, 0:PAR]
        for k in range(1, owners * pairs):
            summed = summed + blocks[phase, k // pairs, k % pairs, :, 0:PAR]
        full[phase, half, :, 0:PAR] = summed
        join = copy(
            full.at[phase, half, :, 0:PAR],
            full.at[phase, half, :, 0:PAR],
            full_send.at[phase],
            full_recv.at[phase],
            sibling,
        )
        join.start()
        join.wait_recv()
        started.extend([swap, join] + sent)
        read = [full[phase, j // width, j % width, 0:PAR] for j in range(shares)]
        empty = jnp.zeros((WIDE - PAR, shares * LANES), jnp.float32)
        return jnp.concatenate([jnp.concatenate(read, axis=1), empty], axis=0)

    def pieces(vector):
        return [vector[:, j * LANES : (j + 1) * LANES] for j in range(shares)]

    gradient = add_up(0, pieces(scatter(weighted)))
    initial_norm = jnp.sqrt(total(gradient * gradient) + epsilon)
    current = gradient / initial_norm
    previous = jnp.zeros_like(gradient)
    beta_term = jnp.zeros((1, 1), jnp.float32)
    diag_terms, off_terms, basis_list = ([], [], [])

    def lay_gradient():
        out_ref[1:2] = in_order(gradient)

    for iteration in range(ITERS):
        terms = pieces(scatter(gather(current)))
        for j, values in enumerate(pieces(current)):
            terms[j] = terms[j] + prior[j] * values
        image_vec = add_up(iteration + 1, terms, None if iteration else lay_gradient)
        alpha_term = total(current * image_vec)
        direction = image_vec - alpha_term * current - beta_term * previous
        beta_next = jnp.sqrt(total(direction * direction) + epsilon)
        diag_terms.append(alpha_term)
        off_terms.append(beta_next)
        basis_list.append(current)
        previous, current, beta_term = (current, direction / beta_next, beta_next)

    first, second = diag_terms
    below, last = off_terms
    corner = first * first + below * below
    side = first * below + below * second
    end = below * below + second * second + last * last
    root = jnp.sqrt(corner)
    lower = side / root
    tip = jnp.sqrt(end - lower * lower)
    forward = initial_norm * first / root
    forward_next = (initial_norm * below - lower * forward) / tip
    back_next = forward_next / tip
    back = (forward - lower * back_next) / root
    result = back * basis_list[0] + back_next * basis_list[1]
    out_ref[0:1] = in_order(result)
    for one in started:
        one.wait_send()


def on_device(
    row_block,
    row_hits,
    row_slot,
    track_kept,
    row_derivs,
    row_resid,
    row_invsig,
    pattern,
    prior,
    owners,
    shares,
):
    args = (
        row_block, row_hits, row_slot, track_kept, row_derivs, row_resid, row_invsig, pattern, prior
    )
    if owners * MODS != shares * LANES or shares % 2:
        return on_device_large(*args)
    rows = row_resid.shape[0]
    dma = pltpu.SemaphoreType.DMA
    tile = (WIDE, LANES)
    width = shares // 2
    out = pl.pallas_call(
        functools.partial(kernel, owners, shares),
        out_shape=jax.ShapeDtypeStruct((2, MODS * PAR), jnp.float32),
        in_specs=[pl.BlockSpec(memory_space=pltpu.HBM)] * 9,
        out_specs=pl.BlockSpec(memory_space=pltpu.VMEM),
        scratch_shapes=[
            pltpu.VMEM((1, rows), jnp.int32),
            pltpu.VMEM((2, rows), jnp.int32),
            pltpu.VMEM((1, rows), jnp.int32),
            pltpu.VMEM((1, track_kept.shape[0]), jnp.int32),
            pltpu.VMEM((2 * PAR, rows), jnp.bfloat16),
            pltpu.VMEM((rows,), jnp.bfloat16),
            pltpu.VMEM((rows,), jnp.bfloat16),
            pltpu.VMEM((1, NB), jnp.int32),
            pltpu.VMEM((1, MODS * PAR), jnp.float32),
            dma((9,)),
            pltpu.VMEM((owners * MODS, 2 * rows), jnp.bfloat16),
            pltpu.VMEM((owners, 1, LANES), jnp.int32),
            pltpu.VMEM((PHASES, 2, width) + tile, jnp.float32),
            pltpu.VMEM((PHASES, width) + tile, jnp.float32),
            pltpu.VMEM((PHASES, owners, shares // 2, width) + tile, jnp.float32),
            pltpu.VMEM((PHASES, 2, width) + tile, jnp.float32),
            dma((owners - 1,)),
            dma((owners - 1,)),
            dma((PHASES,)),
            dma((PHASES,)),
            dma((PHASES, owners, shares // 2)),
            dma((PHASES, owners, shares // 2)),
            dma((PHASES,)),
            dma((PHASES,)),
        ],
        compiler_params=pltpu.CompilerParams(
            collective_id=0, has_side_effects=True, vmem_limit_bytes=60 * 1024 * 1024
        ),
    )(
        row_block.reshape(1, rows),
        row_hits,
        row_slot.reshape(1, rows),
        track_kept.reshape(1, -1),
        row_derivs,
        row_resid,
        row_invsig,
        pattern,
        prior,
    )
    return out[0:1], out[1:2]


def solution(mesh):
    return jax.shard_map(
        functools.partial(on_device, owners=mesh.shape["blk"], shares=mesh.shape["trk"]),
        mesh=mesh,
        in_specs=(
            P(("blk", "trk"), None),
            P(None, ("blk", "trk")),
            P(("blk", "trk")),
            P(("blk", "trk")),
            P(None, ("blk", "trk")),
            P(("blk", "trk")),
            P(("blk", "trk")),
            P("blk", None),
            P("blk", None),
        ),
        out_specs=(P("blk", None), P("blk", None)),
        check_vma=False,
    )
```
